32 devices in a mesh: seq: 2 (over y), fsdp: 16 (over z, x, core).
Axes of the slice: x: 2, y: 2, z: 4, core: 2. Of those that a mesh axis runs over, the one named last changes fastest.
Arguments:
- query: bfloat16 [16, 1024, 3072], P('fsdp', 'seq'), may hold values from -6 to 6
- keys: bfloat16 [16, 1024, 3072], P('fsdp', 'seq'), may hold values from -6 to 6
- values: bfloat16 [16, 1024, 3072], P('fsdp', 'seq'), may hold values from -6 to 6
- hidden_in: bfloat16 [16, 1024, 3072], P('fsdp', 'seq'), may hold values from -6 to 6
- gate: float32 [3072], replicated, may hold values from 0.5 to 2
- out_weight: bfloat16 [3072, 3072], P('seq', 'fsdp'), may hold values from -1.25 to 1.25
- tile_list: int32 [16, 2, 4], P('fsdp'), may hold values from 0 to 31, as said below
- tile_count: int32 [16, 2], P('fsdp'), may hold values from 2 to 4
Outputs:
- block_out: bfloat16 [16, 1024, 3072], P('fsdp', 'seq')
The draws below stay inside these ranges and needn't reach their ends.
Inputs may be any that keep to these rules, and one draw needn't show every extreme that they name: `tile_list`: entry c < tile_count of query tile g names a tile of the span of g or of the span just before or after it (2 tiles a span), live entries of a row are distinct, entry 0 is g itself, and entries at c >= tile_count repeat g.
All inputs are finite; a program needn't handle non-finite values.
Results may differ from the reference program's by a relative error of at most 0.005.
Values may be sent and summed in bfloat16 or wider, within the bound.
No kernel may reach another device: no remote copies, remote signals or barrier semaphores. Data moves between devices by JAX's collectives and lax.ppermute only.
A program may use at most 192 MiB of HBM per device.

```python
import jax
import jax.numpy as jnp
from jax import lax

HEADS = 24
HEAD_DIM = 128
D_OUT = 3072
TILE = 512
KMAX = 4
TILES_C = 2
SPAN = 1024
N_FSDP = 16


def tile_lists(key):
    base = jax.random.fold_in(key, 11)
    key_noise, key_count, key_full, key_least = jax.random.split(base, 4)
    tiles_all = N_FSDP * TILES_C
    spread = 3 * TILES_C
    query_ids = jnp.arange(tiles_all, dtype=jnp.int32)
    span_of = query_ids // TILES_C
    offsets = jnp.arange(spread, dtype=jnp.int32) - TILES_C
    cand_ids = span_of[:, None] * TILES_C + offsets[None, :]
    inside = (cand_ids >= 0) & (cand_ids < tiles_all)
    is_self = cand_ids == query_ids[:, None]
    noise = jax.random.randint(key_noise, (tiles_all, spread), 0, 1 << 20)
    order = jnp.arange(spread, dtype=jnp.int32)[None, :]
    ranking = jnp.where(is_self, 3 * (1 << 26), jnp.where(inside, noise * spread + order + (1 << 26), order))
    picked_rank, picked_at = lax.top_k(ranking, KMAX)
    chosen = jnp.take_along_axis(cand_ids, picked_at, axis=1)
    available = jnp.sum(inside.astype(jnp.int32), axis=1)
    live_count = jnp.minimum(jax.random.randint(key_count, (tiles_all,), 2, KMAX + 1), available)
    full_tile = TILES_C + jax.random.randint(key_full, (), 0, (N_FSDP - 2) * TILES_C)
    least_tile = (full_tile + 1 + jax.random.randint(key_least, (), 0, tiles_all - 1)) % tiles_all
    live_count = jnp.where(query_ids == full_tile, KMAX, live_count)
    live_count = jnp.where(query_ids == least_tile, 2, live_count)
    slot_index = jnp.arange(KMAX, dtype=jnp.int32)[None, :]
    chosen = jnp.where(slot_index < live_count[:, None], chosen, query_ids[:, None])
    return (chosen.reshape(N_FSDP, TILES_C, KMAX).astype(jnp.int32), live_count.reshape(N_FSDP, TILES_C).astype(jnp.int32))


def draw_tile_list(key, part):
    return tile_lists(key)[0]


def draw_tile_count(key, part):
    return tile_lists(key)[1]


def draw_query(key, part):
    shape = (N_FSDP, TILES_C, TILE, HEADS * HEAD_DIM)
    drawn = jnp.clip(jax.random.normal(jax.random.fold_in(key, 1), shape), -6.0, 6.0)
    return drawn.reshape(N_FSDP, TILES_C * TILE, HEADS * HEAD_DIM).astype(jnp.bfloat16)


def draw_keys(key, part):
    shape = (N_FSDP, TILES_C, TILE, HEADS * HEAD_DIM)
    drawn = jnp.clip(jax.random.normal(jax.random.fold_in(key, 2), shape), -6.0, 6.0)
    return drawn.reshape(N_FSDP, TILES_C * TILE, HEADS * HEAD_DIM).astype(jnp.bfloat16)


def block_scale(own_key, dims, cuts, smallest, largest):
    def one(axis_at, parts):
        steps = jax.random.uniform(jax.random.fold_in(jax.random.fold_in(own_key, 6), axis_at), (parts,), jnp.float32, smallest / len(cuts), largest / len(cuts))
        return jnp.repeat(jnp.exp(steps), dims[axis_at] // parts).reshape((-1,) + (1,) * (len(dims) - axis_at - 1))

    factor_of = one(*cuts[0])
    for cut in cuts[1:]:
        factor_of = factor_of * one(*cut)
    return factor_of


def centred(key, extent, scale, limit, pieces=(), held_as=jnp.bfloat16):
    drawn = jax.random.normal(key, extent, jnp.float32) * scale
    if len(pieces) > 0:
        drawn = block_scale(key, extent, pieces, -0.22, 0.18) * drawn
    return jnp.clip(drawn, min=-limit, max=limit).astype(held_as)


def setup_inputs(seed: int = 0) -> dict:
    splits = jax.random.split(jax.random.key(seed), 9)
    query = draw_query(jax.random.fold_in(splits[8], 71), 0)
    keys = draw_keys(jax.random.fold_in(splits[8], 71), 0)
    values = centred(splits[2], (N_FSDP, SPAN, HEADS * HEAD_DIM), 1.0, 6.0, ((0, 16), (1, 2)))
    hidden_in = centred(splits[3], (N_FSDP, SPAN, D_OUT), 1.0, 6.0, ((0, 16), (1, 2)))
    gate = jnp.clip(jax.random.uniform(splits[4], (D_OUT,), jnp.float32, 0.5, 2.0), 0.5, 2.0)
    out_weight = centred(splits[5], (HEADS * HEAD_DIM, D_OUT), HEADS ** -0.5, 1.25, ((0, 2), (1, 16)))
    tile_list = draw_tile_list(jax.random.fold_in(splits[8], 71), 0)
    tile_count = draw_tile_count(jax.random.fold_in(splits[8], 71), 0)
    return dict(query=query, keys=keys, values=values, hidden_in=hidden_in, gate=gate, out_weight=out_weight, tile_list=tile_list, tile_count=tile_count)


def reference(query, keys, values, hidden_in, gate, out_weight, tile_list, tile_count):
    spans_all = query.shape[0]
    span_rows = query.shape[1]
    tiles_all = spans_all * span_rows // TILE
    q_tiles = query.reshape(tiles_all, TILE, HEADS, HEAD_DIM)
    k_tiles = keys.reshape(tiles_all, TILE, HEADS, HEAD_DIM)
    v_tiles = values.reshape(tiles_all, TILE, HEADS, HEAD_DIM)
    key_tiles = tile_list.reshape(tiles_all, KMAX).astype(jnp.int32)
    live_slots = tile_count.reshape(tiles_all).astype(jnp.int32)
    slot_tile = jnp.arange(KMAX * TILE, dtype=jnp.int32) // TILE
    score_scale = 1.0 / (HEAD_DIM ** 0.5)

    def one_tile(operands):
        query_tile, key_ids, live_count = operands
        k_sel = jnp.take(k_tiles, key_ids, axis=0).reshape(KMAX * TILE, HEADS, HEAD_DIM).astype(jnp.float32)
        v_sel = jnp.take(v_tiles, key_ids, axis=0).reshape(KMAX * TILE, HEADS, HEAD_DIM).astype(jnp.float32)
        scores = jnp.einsum("ihd,jhd->hij", query_tile.astype(jnp.float32), k_sel) * score_scale
        usable = (slot_tile < live_count)[None, None, :]
        row_max = jnp.max(jnp.where(usable, scores, -jnp.inf), axis=2, keepdims=True)
        weights = jnp.where(usable, jnp.exp(scores - row_max), 0.0)
        row_total = jnp.sum(weights, axis=2, keepdims=True)
        rounded = weights.astype(jnp.bfloat16).astype(jnp.float32)
        blended = jnp.einsum("hij,jhd->ihd", rounded, v_sel) / jnp.transpose(row_total, (1, 0, 2))
        return blended.astype(jnp.bfloat16).reshape(TILE, HEADS * HEAD_DIM)

    attended = lax.map(one_tile, (q_tiles, key_tiles, live_slots))
    attended = attended.reshape(tiles_all * TILE, HEADS * HEAD_DIM)
    projected = jnp.dot(attended, out_weight, preferred_element_type=jnp.float32)
    residual = hidden_in.reshape(tiles_all * TILE, D_OUT).astype(jnp.float32)
    block_out = (residual + gate[None, :] * projected).astype(jnp.bfloat16)
    return block_out.reshape(spans_all, span_rows, D_OUT)
```

```python
import functools

import jax
import jax.numpy as jnp
from jax import lax
from jax.experimental import pallas as pl
from jax.experimental.pallas import tpu as pltpu
from jax.sharding import PartitionSpec as P

HEAD_DIM = 128
TILE = 512
KMAX = 4
GROUPS = 4
ROWS = 256
VMEM = 60 * 1024 * 1024


def attend_kernel(heads, pieces, picks_ref, count_ref, start_ref, q_ref, *refs):
    kv_refs, (out_ref, k_sel, v_sel) = refs[:pieces], refs[pieces:]
    width = heads * HEAD_DIM
    scale = HEAD_DIM**-0.5 * 1.4426950408889634

    for slot in range(KMAX):
        rows = pl.ds(slot * TILE, TILE)
        for piece in range(pieces):

            @pl.when((picks_ref[slot] == piece) & (slot < count_ref[0]))
            def _():
                k_sel[rows, :] = kv_refs[piece][:, :width]
                v_sel[rows, :] = kv_refs[piece][:, width:]

    for live in range(2, KMAX + 1):

        @pl.when(count_ref[0] == live)
        def _():
            for head in range(heads):
                cols = slice(head * HEAD_DIM, (head + 1) * HEAD_DIM)
                for block in range(TILE // ROWS):
                    rows = slice(block * ROWS, (block + 1) * ROWS)
                    scores = lax.dot_general(
                        q_ref[rows, cols],
                        k_sel[: live * TILE, cols],
                        (((1,), (1,)), ((), ())),
                        preferred_element_type=jnp.float32,
                    )
                    row_max = jnp.max(scores, axis=1, keepdims=True)
                    weights = jnp.exp2((scores - row_max) * scale)
                    total = jnp.sum(weights, axis=1, keepdims=True)
                    blended = jnp.dot(
                        weights.astype(jnp.bfloat16),
                        v_sel[: live * TILE, cols],
                        preferred_element_type=jnp.float32,
                    )
                    out_ref[rows, cols] = (blended / total).astype(jnp.bfloat16)


def attend(queries, column_block, kv_pieces, picks, count):
    width = kv_pieces[0].shape[1] // 2
    heads = width // HEAD_DIM
    pieces = len(kv_pieces)
    whole = pl.BlockSpec((TILE, 2 * width), lambda i, picks, count, start: (0, 0))
    return pl.pallas_call(
        functools.partial(attend_kernel, heads, pieces),
        out_shape=jax.ShapeDtypeStruct((TILE, width), jnp.bfloat16),
        grid_spec=pltpu.PrefetchScalarGridSpec(
            num_scalar_prefetch=3,
            grid=(1,),
            in_specs=[
                pl.BlockSpec((TILE, width), lambda i, picks, count, start: (0, start[0]))
            ]
            + [whole] * pieces,
            out_specs=pl.BlockSpec((TILE, width), lambda i, picks, count, start: (0, 0)),
            scratch_shapes=[
                pltpu.VMEM((KMAX * TILE, width), jnp.bfloat16),
                pltpu.VMEM((KMAX * TILE, width), jnp.bfloat16),
            ],
        ),
        compiler_params=pltpu.CompilerParams(vmem_limit_bytes=VMEM),
        cost_estimate=pl.CostEstimate(
            flops=4 * TILE * KMAX * TILE * width,
            bytes_accessed=2 * TILE * width * (2 * pieces + 2),
            transcendentals=TILE * KMAX * TILE * heads,
        ),
        name="attend",
    )(picks, count, column_block, queries, *kv_pieces)


def project_kernel(parts, groups, hidden_ref, gate_ref, weight_ref, *refs):
    token_refs, out_ref = refs[:-1], refs[-1]
    total = None
    for part in range(parts):
        for group in range(groups):
            tokens = token_refs[part * groups + group]
            width = tokens.shape[1]
            term = lax.dot_general(
                tokens[...],
                weight_ref[part, :, group * width : (group + 1) * width],
                (((1,), (1,)), ((), ())),
                preferred_element_type=jnp.float32,
            )
            total = term if total is None else total + term
    out_ref[...] = (hidden_ref[...].astype(jnp.float32) + gate_ref[...] * total).astype(
        jnp.bfloat16
    )


def project(hidden, gate, weight, tokens, groups):
    parts, channels, depth = weight.shape
    rows = hidden.shape[0]
    block = 512
    return pl.pallas_call(
        functools.partial(project_kernel, parts, groups),
        out_shape=jax.ShapeDtypeStruct((rows, channels), jnp.bfloat16),
        grid=(channels // block,),
        in_specs=[
            pl.BlockSpec((rows, block), lambda j: (0, j)),
            pl.BlockSpec((1, block), lambda j: (0, j)),
            pl.BlockSpec((parts, block, depth), lambda j: (0, j, 0)),
        ]
        + [pl.BlockSpec(t.shape, lambda j: (0, 0)) for t in tokens],
        out_specs=pl.BlockSpec((rows, block), lambda j: (0, j)),
        compiler_params=pltpu.CompilerParams(vmem_limit_bytes=VMEM),
        cost_estimate=pl.CostEstimate(
            flops=2 * rows * channels * parts * depth,
            bytes_accessed=2 * (channels * parts * depth + 3 * rows * channels),
            transcendentals=0,
        ),
        name="project",
    )(hidden, gate, weight, *tokens)


def neighbours(block):
    count = lax.axis_size("fsdp")
    forward = [(i, i + 1) for i in range(count - 1)]
    backward = [(target, source) for source, target in forward]
    return lax.ppermute(block, "fsdp", forward), lax.ppermute(block, "fsdp", backward)


def gathered_weight(out_weight):
    parts = lax.axis_size("seq")
    gathered = lax.all_gather(out_weight.T, ("seq", "fsdp"), axis=0, tiled=True)
    return gathered.reshape(parts, -1, gathered.shape[1])


def pair_attention(query, keys, values, picks, live_slots):
    seat = lax.axis_index("seq")
    half = query.shape[1] // 2
    width = half // GROUPS
    swap = [(0, 1), (1, 0)]

    def cut(array, owner, group):
        return lax.dynamic_slice_in_dim(array, owner * half + group * width, width, axis=1)

    def cut_kv(owner, group):
        return jnp.concatenate([cut(keys, owner, group), cut(values, owner, group)], axis=1)

    place = jnp.asarray(picks, jnp.int32)
    place = (place // 2) * 2 + (place % 2 != seat).astype(jnp.int32)
    mine = lax.dynamic_index_in_dim(place, seat, 0, keepdims=False)
    other = lax.dynamic_index_in_dim(place, 1 - seat, 0, keepdims=False)
    mine_live = lax.dynamic_slice_in_dim(live_slots, seat, 1)
    other_live = lax.dynamic_slice_in_dim(live_slots, 1 - seat, 1)
    low, high = [], []
    for group in range(GROUPS):
        kv_mine = cut_kv(seat, group)
        kv_other = lax.ppermute(cut_kv(1 - seat, group), "seq", swap)
        q_other = lax.ppermute(cut(query, 1 - seat, group), "seq", swap)
        before_mine, after_mine = neighbours(kv_mine)
        before_other, after_other = neighbours(kv_other)
        pieces = [before_mine, before_other, kv_mine, kv_other, after_mine, after_other]
        zero = jnp.zeros((1,), jnp.int32)
        out_other = attend(q_other, zero, pieces, other, other_live)
        out_back = lax.ppermute(out_other, "seq", swap)
        start = (seat * GROUPS + group).astype(jnp.int32).reshape(1)
        out_mine = attend(query, start, pieces, mine, mine_live)
        low.append(jnp.where(seat == 0, out_mine, out_back))
        high.append(jnp.where(seat == 0, out_back, out_mine))
    return low + high


def group_attention(query, keys, values, picks, live_slots):
    parts = lax.axis_size("seq")

    def to_heads(array):
        return lax.all_to_all(array, "seq", split_axis=1, concat_axis=0, tiled=True)

    q_local = to_heads(query)
    kv = jnp.concatenate([to_heads(keys), to_heads(values)], axis=1)
    before, after = neighbours(kv)
    tiles = q_local.shape[0] // TILE
    pieces = [
        lax.slice_in_dim(array, t * TILE, (t + 1) * TILE)
        for array in (before, kv, after)
        for t in range(tiles)
    ]
    zero = jnp.zeros((1,), jnp.int32)
    outs = [
        attend(
            lax.slice_in_dim(q_local, t * TILE, (t + 1) * TILE),
            zero,
            pieces,
            picks[t],
            live_slots[t : t + 1],
        )
        for t in range(tiles)
    ]
    tokens = lax.all_to_all(
        jnp.concatenate(outs, axis=0), "seq", split_axis=0, concat_axis=1, tiled=True
    )
    width = tokens.shape[1] // parts
    return [lax.slice_in_dim(tokens, p * width, (p + 1) * width, axis=1) for p in range(parts)]


def on_device(query, keys, values, hidden_in, gate, out_weight, tile_list, tile_count):
    parts = lax.axis_size("seq")
    tiles = query.shape[1] * parts // TILE
    picks = tile_list[0] - (lax.axis_index("fsdp") - 1) * tiles
    weight = gathered_weight(out_weight)
    paired = parts == 2 and tiles == 2 and query.shape[2] % (2 * GROUPS * HEAD_DIM) == 0
    attention = pair_attention if paired else group_attention
    tokens = attention(query[0], keys[0], values[0], picks, tile_count[0])
    groups = len(tokens) // parts
    return project(hidden_in[0], gate[None, :], weight, tokens, groups)[None]


def solution(mesh):
    return jax.shard_map(
        on_device,
        mesh=mesh,
        in_specs=(
            P("fsdp", "seq", None),
            P("fsdp", "seq", None),
            P("fsdp", "seq", None),
            P("fsdp", "seq", None),
            P(),
            P("seq", "fsdp"),
            P("fsdp", None, None),
            P("fsdp", None),
        ),
        out_specs=P("fsdp", "seq", None),
        check_vma=False,
    )
```

```python
import functools

import jax
import jax.numpy as jnp
from jax import lax
from jax.experimental import pallas as pl
from jax.experimental.pallas import tpu as pltpu
from jax.sharding import PartitionSpec as P

HEAD_DIM = 128
TILE = 512
KMAX = 4
GROUPS = 4
ROWS = 256
VMEM = 60 * 1024 * 1024


def attend_kernel(tiles, heads, pieces, waits, picks_ref, count_ref, column_ref, *refs):
    q_refs, kv_refs = refs[:tiles], refs[tiles : tiles + pieces]
    out_refs, (kv_sel, sems) = refs[tiles + pieces + waits : -2], refs[-2:]
    width = heads * HEAD_DIM
    scale = HEAD_DIM**-0.5 * 1.4426950408889634

    span = kv_refs[0].shape[0] // TILE

    def slot_copy(tile, slot, piece, row):
        return pltpu.make_async_copy(
            kv_refs[piece].at[pl.ds(row, TILE)],
            kv_sel.at[tile, pl.ds(slot * TILE, TILE)],
            sems.at[tile, slot],
        )

    for tile in range(tiles):
        for slot in range(KMAX):
            pick = picks_ref[tile, slot]
            for piece in range(pieces):

                @pl.when((pick // span == piece) & (slot < count_ref[tile]))
                def _():
                    row = pl.multiple_of(lax.rem(pick, span) * TILE, TILE)
                    slot_copy(tile, slot, piece, row).start()

    for tile in range(tiles):
        for slot in range(KMAX):

            @pl.when(slot < count_ref[tile])
            def _():
                slot_copy(tile, slot, 0, 0).wait()

        for live in range(2, KMAX + 1):

            @pl.when(count_ref[tile] == live)
            def _():
                for head in range(heads):
                    cols = slice(head * HEAD_DIM, (head + 1) * HEAD_DIM)
                    v_cols = slice(width + head * HEAD_DIM, width + (head + 1) * HEAD_DIM)
                    for block in range(TILE // ROWS):
                        rows = slice(block * ROWS, (block + 1) * ROWS)
                        scores = lax.dot_general(
                            q_refs[tile][rows, cols],
                            kv_sel[tile, : live * TILE, cols],
                            (((1,), (1,)), ((), ())),
                            preferred_element_type=jnp.float32,
                        )
                        row_max = jnp.max(scores, axis=1, keepdims=True)
                        weights = jnp.exp2((scores - row_max) * scale)
                        total = jnp.sum(weights, axis=1, keepdims=True)
                        blended = jnp.dot(
                            weights.astype(jnp.bfloat16),
                            kv_sel[tile, : live * TILE, v_cols],
                            preferred_element_type=jnp.float32,
                        )
                        out_refs[tile][rows, cols] = (blended / total).astype(jnp.bfloat16)


def attend(queries, columns, kv_pieces, picks, counts, after=()):
    tiles, pieces = len(queries), len(kv_pieces)
    width = kv_pieces[0].shape[1] // 2
    heads = width // HEAD_DIM

    def q_spec(tile):
        return pl.BlockSpec((TILE, width), lambda i, picks, count, column: (0, column[tile]))

    whole = pl.BlockSpec((TILE, width), lambda i, picks, count, column: (0, 0))
    return pl.pallas_call(
        functools.partial(attend_kernel, tiles, heads, pieces, len(after)),
        out_shape=[jax.ShapeDtypeStruct((TILE, width), jnp.bfloat16)] * tiles,
        grid_spec=pltpu.PrefetchScalarGridSpec(
            num_scalar_prefetch=3,
            grid=(1,),
            in_specs=[q_spec(tile) for tile in range(tiles)]
            + [pl.BlockSpec(memory_space=pl.ANY)] * (pieces + len(after)),
            out_specs=[whole] * tiles,
            scratch_shapes=[
                pltpu.VMEM((tiles, KMAX * TILE, 2 * width), jnp.bfloat16),
                pltpu.SemaphoreType.DMA((tiles, KMAX)),
            ],
        ),
        compiler_params=pltpu.CompilerParams(vmem_limit_bytes=VMEM),
        cost_estimate=pl.CostEstimate(
            flops=4 * tiles * TILE * KMAX * TILE * width,
            bytes_accessed=2 * TILE * width * tiles * (2 * KMAX + 2),
            transcendentals=tiles * TILE * KMAX * TILE * heads,
        ),
        name="attend",
    )(picks, counts, columns, *queries, *kv_pieces, *after)


def cut(arrays, columns, width, after=()):
    count, cuts, rows = len(arrays), columns.shape[0], arrays[0].shape[0]

    def kernel(columns_ref, *refs):
        outs = refs[cuts * count + len(after) :]
        for c in range(cuts):
            for n in range(count):
                outs[c][:, n * width : (n + 1) * width] = refs[c * count + n][...]

    def spec(c):
        return pl.BlockSpec((rows, width), lambda i, columns: (0, columns[c]))

    total = width * count
    return pl.pallas_call(
        kernel,
        out_shape=[jax.ShapeDtypeStruct((rows, total), arrays[0].dtype)] * cuts,
        grid_spec=pltpu.PrefetchScalarGridSpec(
            num_scalar_prefetch=1,
            grid=(1,),
            in_specs=[spec(c) for c in range(cuts) for _ in range(count)]
            + [pl.BlockSpec(memory_space=pl.ANY)] * len(after),
            out_specs=[pl.BlockSpec((rows, total), lambda i, columns: (0, 0))] * cuts,
        ),
        compiler_params=pltpu.CompilerParams(vmem_limit_bytes=VMEM),
        cost_estimate=pl.CostEstimate(
            flops=0, bytes_accessed=4 * rows * total * cuts, transcendentals=0
        ),
        name="cut",
    )(columns, *(list(arrays) * cuts), *after)


def project_part(weight, order, tokens, first, groups, last=None):
    parts, channels, _ = weight.shape
    rows, width = tokens[0].shape
    block, depth = 512, groups * width
    extra = [] if last is None else list(last)

    def kernel(order_ref, *refs):
        weight_refs, refs = refs[:parts], refs[parts:]
        token_refs, rest = refs[: len(tokens)], refs[len(tokens) :]
        total = None
        for part in range(parts):
            for group in range(groups):
                term = lax.dot_general(
                    token_refs[part * groups + group][...],
                    weight_refs[part][:, group * width : (group + 1) * width],
                    (((1,), (1,)), ((), ())),
                    preferred_element_type=jnp.float32,
                )
                total = term if total is None else total + term
        if last is None:
            rest[0][...] = total
            return
        hidden_ref, gate_ref = rest[:2]
        if len(rest) == 4:
            total = total + rest[2][...]
        rest[-1][...] = (hidden_ref[...].astype(jnp.float32) + gate_ref[...] * total).astype(
            jnp.bfloat16
        )

    def weight_spec(part):
        return pl.BlockSpec((None, block, depth), lambda j, order: (order[part], j, first // groups))

    kind = jnp.float32 if last is None else jnp.bfloat16
    return pl.pallas_call(
        kernel,
        out_shape=jax.ShapeDtypeStruct((rows, channels), kind),
        grid_spec=pltpu.PrefetchScalarGridSpec(
            num_scalar_prefetch=1,
            grid=(channels // block,),
            in_specs=[weight_spec(part) for part in range(parts)]
            + [pl.BlockSpec(t.shape, lambda j, order: (0, 0)) for t in tokens]
            + [pl.BlockSpec((e.shape[0], block), lambda j, order: (0, j)) for e in extra],
            out_specs=pl.BlockSpec((rows, block), lambda j, order: (0, j)),
        ),
        compiler_params=pltpu.CompilerParams(vmem_limit_bytes=VMEM),
        cost_estimate=pl.CostEstimate(
            flops=2 * rows * channels * parts * depth,
            bytes_accessed=2 * (channels * parts * depth + 3 * rows * channels),
            transcendentals=0,
        ),
        name="project",
    )(order, *([weight] * parts), *tokens, *extra)


def neighbours(block):
    count = lax.axis_size("fsdp")
    forward = [(i, i + 1) for i in range(count - 1)]
    backward = [(target, source) for source, target in forward]
    return lax.ppermute(block, "fsdp", forward), lax.ppermute(block, "fsdp", backward)


def gathered_weight(out_weight):
    parts = lax.axis_size("seq")
    gathered = lax.all_gather(out_weight.T, ("seq", "fsdp"), axis=0, tiled=True)
    return gathered.reshape(parts, -1, gathered.shape[1])


def pair_block(query, keys, values, picks, live_slots, weight, hidden, gate):
    seat = lax.axis_index("seq").astype(jnp.int32)
    half = query.shape[1] // 2
    width = half // GROUPS
    swap = [(0, 1), (1, 0)]
    order = jnp.stack([seat, 1 - seat])

    place = (picks // 2) * 2 + (picks % 2 != seat).astype(jnp.int32)
    place = jnp.where(seat == 0, place[::-1], place)
    counts = jnp.where(seat == 0, live_slots[::-1], live_slots)
    arrived, mine, back = [], [], []
    depth = GROUPS // 2
    for group in range(GROUPS):
        columns = order * GROUPS + group
        kv_mine, kv_send = cut([keys, values], columns, width, (arrived[group - 2],) if group >= 2 else ())
        kv_other = lax.ppermute(kv_send, "seq", swap)
        arrived.append(kv_other)
        kv_span = jnp.concatenate([kv_mine, kv_other], axis=0)
        before, after = neighbours(kv_span)
        pieces = [before, kv_span, after]
        after = (kv_other,) if group == 0 else (mine[-1],)
        (q_send,) = cut([query], columns[1:], width, after)
        q_other = lax.ppermute(q_send, "seq", swap)
        starts = jnp.stack([jnp.zeros_like(seat), columns[0]])
        out_other, out_mine = attend([q_other, query], starts, pieces, place, counts)
        mine.append(out_mine)
        back.append(lax.ppermute(out_other, "seq", swap))
    partial = project_part(weight, order, mine[:depth] + back[:depth], 0, depth)
    tokens = mine[depth:] + back[depth:]
    return project_part(weight, order, tokens, depth, depth, (hidden, gate, partial))


def group_block(query, keys, values, picks, live_slots, weight, hidden, gate):
    parts = lax.axis_size("seq")

    def to_heads(array):
        return lax.all_to_all(array, "seq", split_axis=1, concat_axis=0, tiled=True)

    q_local = to_heads(query)
    kv = jnp.concatenate([to_heads(keys), to_heads(values)], axis=1)
    before, after = neighbours(kv)
    tiles = q_local.shape[0] // TILE
    pieces = [before, kv, after]
    queries = [lax.slice_in_dim(q_local, t * TILE, (t + 1) * TILE) for t in range(tiles)]
    outs = attend(queries, jnp.zeros((tiles,), jnp.int32), pieces, picks, live_slots)
    tokens = lax.all_to_all(
        jnp.concatenate(outs, axis=0), "seq", split_axis=0, concat_axis=1, tiled=True
    )
    width = tokens.shape[1] // parts
    tokens = [lax.slice_in_dim(tokens, p * width, (p + 1) * width, axis=1) for p in range(parts)]
    return project_part(weight, jnp.arange(parts, dtype=jnp.int32), tokens, 0, 1, (hidden, gate))


def on_device(query, keys, values, hidden_in, gate, out_weight, tile_list, tile_count):
    parts = lax.axis_size("seq")
    tiles = query.shape[1] * parts // TILE
    picks = tile_list[0] - (lax.axis_index("fsdp") - 1) * tiles
    paired = parts == 2 and tiles == 2 and query.shape[2] % (2 * GROUPS * HEAD_DIM) == 0
    weight = gathered_weight(out_weight)
    block = pair_block if paired else group_block
    out = block(
        query[0], keys[0], values[0], picks, tile_count[0], weight, hidden_in[0], gate[None, :]
    )
    return out[None]


def solution(mesh):
    return jax.shard_map(
        on_device,
        mesh=mesh,
        in_specs=(
            P("fsdp", "seq", None),
            P("fsdp", "seq", None),
            P("fsdp", "seq", None),
            P("fsdp", "seq", None),
            P(),
            P("seq", "fsdp"),
            P("fsdp", None, None),
            P("fsdp", None),
        ),
        out_specs=P("fsdp", "seq", None),
        check_vma=False,
    )
```

```python
import functools

import jax
import jax.numpy as jnp
from jax import lax
from jax.experimental import pallas as pl
from jax.experimental.pallas import tpu as pltpu
from jax.sharding import PartitionSpec as P

HEAD_DIM = 128
TILE = 512
KMAX = 4
GROUPS = 4
SPLIT = 1
ROWS = 256
VMEM = 60 * 1024 * 1024


def attend_kernel(tiles, heads, pieces, sources, waits, picks_ref, count_ref, column_ref, *refs):
    q_refs, kv_refs = refs[:tiles], refs[tiles : tiles + pieces]
    out_refs, (kv_sel, sems) = refs[tiles + pieces + waits : -2], refs[-2:]
    width = heads * HEAD_DIM
    scale = HEAD_DIM**-0.5 * 1.4426950408889634


    def slot_copy(tile, slot, piece):
        array, row = sources[piece]
        return pltpu.make_async_copy(
            kv_refs[array].at[pl.ds(row, TILE)],
            kv_sel.at[tile, pl.ds(slot * TILE, TILE)],
            sems.at[tile, slot],
        )

    for tile in range(tiles):
        for slot in range(KMAX):
            for piece in range(len(sources)):

                @pl.when((picks_ref[tile, slot] == piece) & (slot < count_ref[tile]))
                def _():
                    slot_copy(tile, slot, piece).start()

    for tile in range(tiles):
        for slot in range(KMAX):

            @pl.when(slot < count_ref[tile])
            def _():
                slot_copy(tile, slot, 0).wait()

        for live in range(2, KMAX + 1):

            @pl.when(count_ref[tile] == live)
            def _():
                for head in range(heads):
                    cols = slice(head * HEAD_DIM, (head + 1) * HEAD_DIM)
                    v_cols = slice(width + head * HEAD_DIM, width + (head + 1) * HEAD_DIM)
                    for block in range(TILE // ROWS):
                        rows = slice(block * ROWS, (block + 1) * ROWS)
                        scores = lax.dot_general(
                            q_refs[tile][rows, cols],
                            kv_sel[tile, : live * TILE, cols],
                            (((1,), (1,)), ((), ())),
                            preferred_element_type=jnp.float32,
                        )
                        row_max = jnp.max(scores, axis=1, keepdims=True)
                        weights = jnp.exp2((scores - row_max) * scale)
                        total = jnp.sum(weights, axis=1, keepdims=True)
                        blended = jnp.dot(
                            weights.astype(jnp.bfloat16),
                            kv_sel[tile, : live * TILE, v_cols],
                            preferred_element_type=jnp.float32,
                        )
                        out_refs[tile][rows, cols] = (blended / total).astype(jnp.bfloat16)


def attend(queries, columns, kv_pieces, picks, counts, after=()):
    tiles, pieces = len(queries), len(kv_pieces)
    sources = [
        (n, row) for n, piece in enumerate(kv_pieces) for row in range(0, piece.shape[0], TILE)
    ]
    width = kv_pieces[0].shape[1] // 2
    heads = width // HEAD_DIM

    def q_spec(tile):
        return pl.BlockSpec((TILE, width), lambda i, picks, count, column: (0, column[tile]))

    whole = pl.BlockSpec((TILE, width), lambda i, picks, count, column: (0, 0))
    return pl.pallas_call(
        functools.partial(attend_kernel, tiles, heads, pieces, sources, len(after)),
        out_shape=[jax.ShapeDtypeStruct((TILE, width), jnp.bfloat16)] * tiles,
        grid_spec=pltpu.PrefetchScalarGridSpec(
            num_scalar_prefetch=3,
            grid=(1,),
            in_specs=[q_spec(tile) for tile in range(tiles)]
            + [pl.BlockSpec(memory_space=pl.ANY)] * (pieces + len(after)),
            out_specs=[whole] * tiles,
            scratch_shapes=[
                pltpu.VMEM((tiles, KMAX * TILE, 2 * width), jnp.bfloat16),
                pltpu.SemaphoreType.DMA((tiles, KMAX)),
            ],
        ),
        compiler_params=pltpu.CompilerParams(vmem_limit_bytes=VMEM),
        cost_estimate=pl.CostEstimate(
            flops=4 * tiles * TILE * KMAX * TILE * width,
            bytes_accessed=2 * TILE * width * tiles * (2 * KMAX + 2),
            transcendentals=tiles * TILE * KMAX * TILE * heads,
        ),
        name="attend",
    )(picks, counts, columns, *queries, *kv_pieces, *after)


def cut(arrays, columns, width, after=()):
    count, cuts, rows = len(arrays), columns.shape[0], arrays[0].shape[0]

    def kernel(columns_ref, *refs):
        outs = refs[cuts * count + len(after) :]
        for c in range(cuts):
            for n in range(count):
                outs[c][:, n * width : (n + 1) * width] = refs[c * count + n][...]

    def spec(c):
        return pl.BlockSpec((rows, width), lambda i, columns: (0, columns[c]))

    total = width * count
    return pl.pallas_call(
        kernel,
        out_shape=[jax.ShapeDtypeStruct((rows, total), arrays[0].dtype)] * cuts,
        grid_spec=pltpu.PrefetchScalarGridSpec(
            num_scalar_prefetch=1,
            grid=(1,),
            in_specs=[spec(c) for c in range(cuts) for _ in range(count)]
            + [pl.BlockSpec(memory_space=pl.ANY)] * len(after),
            out_specs=[pl.BlockSpec((rows, total), lambda i, columns: (0, 0))] * cuts,
        ),
        compiler_params=pltpu.CompilerParams(vmem_limit_bytes=VMEM),
        cost_estimate=pl.CostEstimate(
            flops=0, bytes_accessed=4 * rows * total * cuts, transcendentals=0
        ),
        name="cut",
    )(columns, *(list(arrays) * cuts), *after)


def project(weight, order, tokens, hidden, gate):
    parts, channels, depth = weight.shape
    rows = hidden.shape[0]
    block, each = 512, len(tokens) // parts

    def kernel(order_ref, *refs):
        weight_refs, token_refs = refs[:parts], refs[parts : parts + len(tokens)]
        hidden_ref, gate_ref, out_ref = refs[parts + len(tokens) :]
        total = None
        for part in range(parts):
            mine = [ref[...] for ref in token_refs[part * each : (part + 1) * each]]
            term = lax.dot_general(
                mine[0] if each == 1 else jnp.concatenate(mine, axis=1),
                weight_refs[part][...],
                (((1,), (1,)), ((), ())),
                preferred_element_type=jnp.float32,
            )
            total = term if total is None else total + term
        out_ref[...] = (hidden_ref[...].astype(jnp.float32) + gate_ref[...] * total).astype(
            jnp.bfloat16
        )

    def weight_spec(part):
        return pl.BlockSpec((None, block, depth), lambda j, order: (order[part], j, 0))

    return pl.pallas_call(
        kernel,
        out_shape=jax.ShapeDtypeStruct((rows, channels), jnp.bfloat16),
        grid_spec=pltpu.PrefetchScalarGridSpec(
            num_scalar_prefetch=1,
            grid=(channels // block,),
            in_specs=[weight_spec(part) for part in range(parts)]
            + [pl.BlockSpec(t.shape, lambda j, order: (0, 0)) for t in tokens]
            + [
                pl.BlockSpec((rows, block), lambda j, order: (0, j)),
                pl.BlockSpec((1, block), lambda j, order: (0, j)),
            ],
            out_specs=pl.BlockSpec((rows, block), lambda j, order: (0, j)),
        ),
        compiler_params=pltpu.CompilerParams(vmem_limit_bytes=VMEM),
        cost_estimate=pl.CostEstimate(
            flops=2 * rows * channels * parts * depth,
            bytes_accessed=2 * (channels * parts * depth + 3 * rows * channels),
            transcendentals=0,
        ),
        name="project",
    )(order, *([weight] * parts), *tokens, hidden, gate)


def neighbours(block):
    count = lax.axis_size("fsdp")
    forward = [(i, i + 1) for i in range(count - 1)]
    backward = [(target, source) for source, target in forward]
    return lax.ppermute(block, "fsdp", forward), lax.ppermute(block, "fsdp", backward)


def gathered_weight(out_weight):
    parts = lax.axis_size("seq")
    gathered = lax.all_gather(out_weight.T, ("seq", "fsdp"), axis=0, tiled=True)
    return gathered.reshape(parts, -1, gathered.shape[1])


def pair_block(query, keys, values, picks, live_slots, weight, hidden, gate):
    seat = lax.axis_index("seq").astype(jnp.int32)
    half = query.shape[1] // 2
    width = half // GROUPS
    swap = [(0, 1), (1, 0)]
    order = jnp.stack([seat, 1 - seat])

    place = (picks // 2) * 2 + (picks % 2 != seat).astype(jnp.int32)
    place = jnp.where(seat == 0, place[::-1], place)
    counts = jnp.where(seat == 0, live_slots[::-1], live_slots)
    arrived, mine, back = [], [], []
    zero = jnp.zeros((1,), jnp.int32)
    before_q = ()
    for group in range(GROUPS):
        columns = order * GROUPS + group
        after = (arrived[group - 2],) if group >= 2 else ()
        kv_mine, kv_send = cut([keys, values], columns, width, after)
        kv_other = lax.ppermute(kv_send, "seq", swap)
        arrived.append(kv_other)
        if group < SPLIT:
            before_mine, after_mine = neighbours(kv_mine)
            before_other, after_other = neighbours(kv_other)
            pieces = [before_mine, before_other, kv_mine, kv_other, after_mine, after_other]
        else:
            kv_span = jnp.concatenate([kv_mine, kv_other], axis=0)
            span_before, span_after = neighbours(kv_span)
            pieces = [span_before, kv_span, span_after]
        (q_send,) = cut([query], columns[1:], width, before_q if group else (kv_other,))
        q_other = lax.ppermute(q_send, "seq", swap)
        (out_other,) = attend([q_other], zero, pieces, place[:1], counts[:1], tuple(mine[-1:]))
        back.append(lax.ppermute(out_other, "seq", swap))
        before_q = (out_other,)
        (out_mine,) = attend(
            [query], columns[:1], pieces, place[1:], counts[1:], (out_other,)
        )
        mine.append(out_mine)
    return project(weight, order, mine + back, hidden, gate)


def group_block(query, keys, values, picks, live_slots, weight, hidden, gate):
    parts = lax.axis_size("seq")

    def to_heads(array):
        return lax.all_to_all(array, "seq", split_axis=1, concat_axis=0, tiled=True)

    q_local = to_heads(query)
    kv = jnp.concatenate([to_heads(keys), to_heads(values)], axis=1)
    before, after = neighbours(kv)
    tiles = q_local.shape[0] // TILE
    pieces = [before, kv, after]
    queries = [lax.slice_in_dim(q_local, t * TILE, (t + 1) * TILE) for t in range(tiles)]
    outs = attend(queries, jnp.zeros((tiles,), jnp.int32), pieces, picks, live_slots)
    tokens = lax.all_to_all(
        jnp.concatenate(outs, axis=0), "seq", split_axis=0, concat_axis=1, tiled=True
    )
    width = tokens.shape[1] // parts
    tokens = [lax.slice_in_dim(tokens, p * width, (p + 1) * width, axis=1) for p in range(parts)]
    return project(weight, jnp.arange(parts, dtype=jnp.int32), tokens, hidden, gate)


def on_device(query, keys, values, hidden_in, gate, out_weight, tile_list, tile_count):
    parts = lax.axis_size("seq")
    tiles = query.shape[1] * parts // TILE
    picks = tile_list[0] - (lax.axis_index("fsdp") - 1) * tiles
    paired = parts == 2 and tiles == 2 and query.shape[2] % (2 * GROUPS * HEAD_DIM) == 0
    weight = gathered_weight(out_weight)
    block = pair_block if paired else group_block
    out = block(
        query[0], keys[0], values[0], picks, tile_count[0], weight, hidden_in[0], gate[None, :]
    )
    return out[None]


def solution(mesh):
    return jax.shard_map(
        on_device,
        mesh=mesh,
        in_specs=(
            P("fsdp", "seq", None),
            P("fsdp", "seq", None),
            P("fsdp", "seq", None),
            P("fsdp", "seq", None),
            P(),
            P("seq", "fsdp"),
            P("fsdp", None, None),
            P("fsdp", None),
        ),
        out_specs=P("fsdp", "seq", None),
        check_vma=False,
    )
```

```python
import functools

import jax
import jax.numpy as jnp
from jax import lax
from jax.experimental import pallas as pl
from jax.experimental.pallas import tpu as pltpu
from jax.sharding import PartitionSpec as P

HEAD_DIM = 128
TILE = 512
KMAX = 4
GROUPS = 4
SPLIT = 1
ROWS = 256
VMEM = 60 * 1024 * 1024


def attend_kernel(tiles, heads, pieces, sources, waits, picks_ref, count_ref, column_ref, *refs):
    q_refs, kv_refs = refs[:tiles], refs[tiles : tiles + pieces]
    out_refs, (kv_sel, sems) = refs[tiles + pieces + waits : -2], refs[-2:]
    width = heads * HEAD_DIM
    scale = HEAD_DIM**-0.5 * 1.4426950408889634


    def slot_copy(tile, slot, piece):
        array, row = sources[piece]
        return pltpu.make_async_copy(
            kv_refs[array].at[pl.ds(row, TILE)],
            kv_sel.at[tile, pl.ds(slot * TILE, TILE)],
            sems.at[tile, slot],
        )

    for tile in range(tiles):
        for slot in range(KMAX):
            for piece in range(len(sources)):

                @pl.when((picks_ref[tile, slot] == piece) & (slot < count_ref[tile]))
                def _():
                    slot_copy(tile, slot, piece).start()

    for tile in range(tiles):
        for slot in range(KMAX):

            @pl.when(slot < count_ref[tile])
            def _():
                slot_copy(tile, slot, 0).wait()

        for live in range(2, KMAX + 1):

            @pl.when(count_ref[tile] == live)
            def _():
                for head in range(heads):
                    cols = slice(head * HEAD_DIM, (head + 1) * HEAD_DIM)
                    v_cols = slice(width + head * HEAD_DIM, width + (head + 1) * HEAD_DIM)
                    for block in range(TILE // ROWS):
                        rows = slice(block * ROWS, (block + 1) * ROWS)
                        scores = lax.dot_general(
                            q_refs[tile][rows, cols],
                            kv_sel[tile, : live * TILE, cols],
                            (((1,), (1,)), ((), ())),
                            preferred_element_type=jnp.float32,
                        )
                        row_max = jnp.max(scores, axis=1, keepdims=True)
                        weights = jnp.exp2((scores - row_max) * scale)
                        total = jnp.sum(weights, axis=1, keepdims=True)
                        blended = jnp.dot(
                            weights.astype(jnp.bfloat16),
                            kv_sel[tile, : live * TILE, v_cols],
                            preferred_element_type=jnp.float32,
                        )
                        out_refs[tile][rows, cols] = (blended / total).astype(jnp.bfloat16)


def attend(queries, columns, kv_pieces, picks, counts, after=()):
    tiles, pieces = len(queries), len(kv_pieces)
    sources = [
        (n, row) for n, piece in enumerate(kv_pieces) for row in range(0, piece.shape[0], TILE)
    ]
    width = kv_pieces[0].shape[1] // 2
    heads = width // HEAD_DIM

    def q_spec(tile):
        return pl.BlockSpec((TILE, width), lambda i, picks, count, column: (0, column[tile]))

    whole = pl.BlockSpec((TILE, width), lambda i, picks, count, column: (0, 0))
    return pl.pallas_call(
        functools.partial(attend_kernel, tiles, heads, pieces, sources, len(after)),
        out_shape=[jax.ShapeDtypeStruct((TILE, width), jnp.bfloat16)] * tiles,
        grid_spec=pltpu.PrefetchScalarGridSpec(
            num_scalar_prefetch=3,
            grid=(1,),
            in_specs=[q_spec(tile) for tile in range(tiles)]
            + [pl.BlockSpec(memory_space=pl.ANY)] * (pieces + len(after)),
            out_specs=[whole] * tiles,
            scratch_shapes=[
                pltpu.VMEM((tiles, KMAX * TILE, 2 * width), jnp.bfloat16),
                pltpu.SemaphoreType.DMA((tiles, KMAX)),
            ],
        ),
        compiler_params=pltpu.CompilerParams(vmem_limit_bytes=VMEM),
        cost_estimate=pl.CostEstimate(
            flops=4 * tiles * TILE * KMAX * TILE * width,
            bytes_accessed=2 * TILE * width * tiles * (2 * KMAX + 2),
            transcendentals=tiles * TILE * KMAX * TILE * heads,
        ),
        name="attend",
    )(picks, counts, columns, *queries, *kv_pieces, *after)


def cut(arrays, columns, width, after=()):
    count, cuts, rows = len(arrays), columns.shape[0], arrays[0].shape[0]

    def kernel(columns_ref, *refs):
        outs = refs[cuts * count + len(after) :]
        for c in range(cuts):
            for n in range(count):
                outs[c][:, n * width : (n + 1) * width] = refs[c * count + n][...]

    def spec(c):
        return pl.BlockSpec((rows, width), lambda i, columns: (0, columns[c]))

    total = width * count
    return pl.pallas_call(
        kernel,
        out_shape=[jax.ShapeDtypeStruct((rows, total), arrays[0].dtype)] * cuts,
        grid_spec=pltpu.PrefetchScalarGridSpec(
            num_scalar_prefetch=1,
            grid=(1,),
            in_specs=[spec(c) for c in range(cuts) for _ in range(count)]
            + [pl.BlockSpec(memory_space=pl.ANY)] * len(after),
            out_specs=[pl.BlockSpec((rows, total), lambda i, columns: (0, 0))] * cuts,
        ),
        compiler_params=pltpu.CompilerParams(vmem_limit_bytes=VMEM),
        cost_estimate=pl.CostEstimate(
            flops=0, bytes_accessed=4 * rows * total * cuts, transcendentals=0
        ),
        name="cut",
    )(columns, *(list(arrays) * cuts), *after)


def join(first, second, after=()):
    rows, width = first.shape

    def kernel(first_ref, second_ref, *refs):
        refs[-1][:rows] = first_ref[...]
        refs[-1][rows:] = second_ref[...]

    return pl.pallas_call(
        kernel,
        out_shape=jax.ShapeDtypeStruct((2 * rows, width), first.dtype),
        in_specs=[pl.BlockSpec(memory_space=pltpu.VMEM)] * 2
        + [pl.BlockSpec(memory_space=pl.ANY)] * len(after),
        out_specs=pl.BlockSpec(memory_space=pltpu.VMEM),
        compiler_params=pltpu.CompilerParams(vmem_limit_bytes=VMEM),
        cost_estimate=pl.CostEstimate(
            flops=0, bytes_accessed=8 * rows * width, transcendentals=0
        ),
        name="join",
    )(first, second, *after)


def project(weight, order, tokens, hidden, gate):
    parts, channels, depth = weight.shape
    rows = hidden.shape[0]
    block, each = 512, len(tokens) // parts

    def kernel(order_ref, *refs):
        weight_refs, token_refs = refs[:parts], refs[parts : parts + len(tokens)]
        hidden_ref, gate_ref, out_ref = refs[parts + len(tokens) :]
        total = None
        for part in range(parts):
            mine = [ref[...] for ref in token_refs[part * each : (part + 1) * each]]
            term = lax.dot_general(
                mine[0] if each == 1 else jnp.concatenate(mine, axis=1),
                weight_refs[part][...],
                (((1,), (1,)), ((), ())),
                preferred_element_type=jnp.float32,
            )
            total = term if total is None else total + term
        out_ref[...] = (hidden_ref[...].astype(jnp.float32) + gate_ref[...] * total).astype(
            jnp.bfloat16
        )

    def weight_spec(part):
        return pl.BlockSpec((None, block, depth), lambda j, order: (order[part], j, 0))

    return pl.pallas_call(
        kernel,
        out_shape=jax.ShapeDtypeStruct((rows, channels), jnp.bfloat16),
        grid_spec=pltpu.PrefetchScalarGridSpec(
            num_scalar_prefetch=1,
            grid=(channels // block,),
            in_specs=[weight_spec(part) for part in range(parts)]
            + [pl.BlockSpec(t.shape, lambda j, order: (0, 0)) for t in tokens]
            + [
                pl.BlockSpec((rows, block), lambda j, order: (0, j)),
                pl.BlockSpec((1, block), lambda j, order: (0, j)),
            ],
            out_specs=pl.BlockSpec((rows, block), lambda j, order: (0, j)),
        ),
        compiler_params=pltpu.CompilerParams(vmem_limit_bytes=VMEM),
        cost_estimate=pl.CostEstimate(
            flops=2 * rows * channels * parts * depth,
            bytes_accessed=2 * (channels * parts * depth + 3 * rows * channels),
            transcendentals=0,
        ),
        name="project",
    )(order, *([weight] * parts), *tokens, hidden, gate)


def neighbours(block):
    count = lax.axis_size("fsdp")
    forward = [(i, i + 1) for i in range(count - 1)]
    backward = [(target, source) for source, target in forward]
    return lax.ppermute(block, "fsdp", forward), lax.ppermute(block, "fsdp", backward)


def gathered_weight(out_weight):
    parts = lax.axis_size("seq")
    gathered = lax.all_gather(out_weight.T, ("seq", "fsdp"), axis=0, tiled=True)
    return gathered.reshape(parts, -1, gathered.shape[1])


def pair_block(query, keys, values, picks, live_slots, weight, hidden, gate):
    seat = lax.axis_index("seq").astype(jnp.int32)
    half = query.shape[1] // 2
    width = half // GROUPS
    swap = [(0, 1), (1, 0)]
    order = jnp.stack([seat, 1 - seat])

    place = (picks // 2) * 2 + (picks % 2 != seat).astype(jnp.int32)
    place = jnp.where(seat == 0, place[::-1], place)
    counts = jnp.where(seat == 0, live_slots[::-1], live_slots)
    arrived, theirs, mine, back = [], [], [], []
    zero = jnp.zeros((1,), jnp.int32)
    for group in range(GROUPS):
        columns = order * GROUPS + group
        after = (arrived[group - 2],) if group >= 2 else ()
        kv_mine, kv_send = cut([keys, values], columns, width, after)
        kv_other = lax.ppermute(kv_send, "seq", swap)
        arrived.append(kv_other)
        if group < SPLIT:
            before_mine, after_mine = neighbours(kv_mine)
            before_other, after_other = neighbours(kv_other)
            pieces = [before_mine, before_other, kv_mine, kv_other, after_mine, after_other]
        else:
            kv_span = join(kv_mine, kv_other, (theirs[group - 2],) if group >= 2 else ())
            span_before, span_after = neighbours(kv_span)
            pieces = [span_before, kv_span, span_after]
        last = group == GROUPS - 1
        (q_send,) = cut([query], columns[1:], width, (theirs[-1] if last else kv_other,))
        q_other = lax.ppermute(q_send, "seq", swap)
        after = tuple(mine[-1:]) + tuple(back[group - 2 : group - 1] if group >= 2 else ())
        (out_other,) = attend([q_other], zero, pieces, place[:1], counts[:1], after)
        back.append(lax.ppermute(out_other, "seq", swap))
        theirs.append(out_other)
        (out_mine,) = attend(
            [query], columns[:1], pieces, place[1:], counts[1:], (out_other,)
        )
        mine.append(out_mine)
    return project(weight, order, mine + back, hidden, gate)


def group_block(query, keys, values, picks, live_slots, weight, hidden, gate):
    parts = lax.axis_size("seq")

    def to_heads(array):
        return lax.all_to_all(array, "seq", split_axis=1, concat_axis=0, tiled=True)

    q_local = to_heads(query)
    kv = jnp.concatenate([to_heads(keys), to_heads(values)], axis=1)
    before, after = neighbours(kv)
    tiles = q_local.shape[0] // TILE
    pieces = [before, kv, after]
    queries = [lax.slice_in_dim(q_local, t * TILE, (t + 1) * TILE) for t in range(tiles)]
    outs = attend(queries, jnp.zeros((tiles,), jnp.int32), pieces, picks, live_slots)
    tokens = lax.all_to_all(
        jnp.concatenate(outs, axis=0), "seq", split_axis=0, concat_axis=1, tiled=True
    )
    width = tokens.shape[1] // parts
    tokens = [lax.slice_in_dim(tokens, p * width, (p + 1) * width, axis=1) for p in range(parts)]
    return project(weight, jnp.arange(parts, dtype=jnp.int32), tokens, hidden, gate)


def on_device(query, keys, values, hidden_in, gate, out_weight, tile_list, tile_count):
    parts = lax.axis_size("seq")
    tiles = query.shape[1] * parts // TILE
    picks = tile_list[0] - (lax.axis_index("fsdp") - 1) * tiles
    paired = parts == 2 and tiles == 2 and query.shape[2] % (2 * GROUPS * HEAD_DIM) == 0
    weight = gathered_weight(out_weight)
    block = pair_block if paired else group_block
    out = block(
        query[0], keys[0], values[0], picks, tile_count[0], weight, hidden_in[0], gate[None, :]
    )
    return out[None]


def solution(mesh):
    return jax.shard_map(
        on_device,
        mesh=mesh,
        in_specs=(
            P("fsdp", "seq", None),
            P("fsdp", "seq", None),
            P("fsdp", "seq", None),
            P("fsdp", "seq", None),
            P(),
            P("seq", "fsdp"),
            P("fsdp", None, None),
            P("fsdp", None),
        ),
        out_specs=P("fsdp", "seq", None),
        check_vma=False,
    )
```

```python
import functools

import jax
import jax.numpy as jnp
from jax import lax
from jax.experimental import pallas as pl
from jax.experimental.pallas import tpu as pltpu
from jax.sharding import PartitionSpec as P

HEAD_DIM = 128
TILE = 512
KMAX = 4
GROUPS = 4
SPLIT = 2
ROWS = 256
VMEM = 60 * 1024 * 1024


def attend_kernel(tiles, heads, pieces, sources, waits, picks_ref, count_ref, column_ref, *refs):
    q_refs, kv_refs = refs[:tiles], refs[tiles : tiles + pieces]
    out_refs, (kv_sel, sems) = refs[tiles + pieces + waits : -2], refs[-2:]
    width = heads * HEAD_DIM
    scale = HEAD_DIM**-0.5 * 1.4426950408889634


    def slot_copy(tile, slot, piece):
        array, row = sources[piece]
        return pltpu.make_async_copy(
            kv_refs[array].at[pl.ds(row, TILE)],
            kv_sel.at[tile, pl.ds(slot * TILE, TILE)],
            sems.at[tile, slot],
        )

    for tile in range(tiles):
        for slot in range(KMAX):
            for piece in range(len(sources)):

                @pl.when((picks_ref[tile, slot] == piece) & (slot < count_ref[tile]))
                def _():
                    slot_copy(tile, slot, piece).start()

    for tile in range(tiles):
        for slot in range(KMAX):

            @pl.when(slot < count_ref[tile])
            def _():
                slot_copy(tile, slot, 0).wait()

        for live in range(2, KMAX + 1):

            @pl.when(count_ref[tile] == live)
            def _():
                for head in range(heads):
                    cols = slice(head * HEAD_DIM, (head + 1) * HEAD_DIM)
                    v_cols = slice(width + head * HEAD_DIM, width + (head + 1) * HEAD_DIM)
                    for block in range(TILE // ROWS):
                        rows = slice(block * ROWS, (block + 1) * ROWS)
                        scores = lax.dot_general(
                            q_refs[tile][rows, cols],
                            kv_sel[tile, : live * TILE, cols],
                            (((1,), (1,)), ((), ())),
                            preferred_element_type=jnp.float32,
                        )
                        row_max = jnp.max(scores, axis=1, keepdims=True)
                        weights = jnp.exp2((scores - row_max) * scale)
                        total = jnp.sum(weights, axis=1, keepdims=True)
                        blended = jnp.dot(
                            weights.astype(jnp.bfloat16),
                            kv_sel[tile, : live * TILE, v_cols],
                            preferred_element_type=jnp.float32,
                        )
                        out_refs[tile][rows, cols] = (blended / total).astype(jnp.bfloat16)


def attend(queries, columns, kv_pieces, picks, counts, after=()):
    tiles, pieces = len(queries), len(kv_pieces)
    sources = [
        (n, row) for n, piece in enumerate(kv_pieces) for row in range(0, piece.shape[0], TILE)
    ]
    width = kv_pieces[0].shape[1] // 2
    heads = width // HEAD_DIM

    def q_spec(tile):
        return pl.BlockSpec((TILE, width), lambda i, picks, count, column: (0, column[tile]))

    whole = pl.BlockSpec((TILE, width), lambda i, picks, count, column: (0, 0))
    return pl.pallas_call(
        functools.partial(attend_kernel, tiles, heads, pieces, sources, len(after)),
        out_shape=[jax.ShapeDtypeStruct((TILE, width), jnp.bfloat16)] * tiles,
        grid_spec=pltpu.PrefetchScalarGridSpec(
            num_scalar_prefetch=3,
            grid=(1,),
            in_specs=[q_spec(tile) for tile in range(tiles)]
            + [pl.BlockSpec(memory_space=pl.ANY)] * (pieces + len(after)),
            out_specs=[whole] * tiles,
            scratch_shapes=[
                pltpu.VMEM((tiles, KMAX * TILE, 2 * width), jnp.bfloat16),
                pltpu.SemaphoreType.DMA((tiles, KMAX)),
            ],
        ),
        compiler_params=pltpu.CompilerParams(vmem_limit_bytes=VMEM),
        cost_estimate=pl.CostEstimate(
            flops=4 * tiles * TILE * KMAX * TILE * width,
            bytes_accessed=2 * TILE * width * tiles * (2 * KMAX + 2),
            transcendentals=tiles * TILE * KMAX * TILE * heads,
        ),
        name="attend",
    )(picks, counts, columns, *queries, *kv_pieces, *after)


def cut(arrays, columns, width, after=()):
    count, cuts, rows = len(arrays), columns.shape[0], arrays[0].shape[0]

    def kernel(columns_ref, *refs):
        outs = refs[cuts * count + len(after) :]
        for c in range(cuts):
            for n in range(count):
                outs[c][:, n * width : (n + 1) * width] = refs[c * count + n][...]

    def spec(c):
        return pl.BlockSpec((rows, width), lambda i, columns: (0, columns[c]))

    total = width * count
    return pl.pallas_call(
        kernel,
        out_shape=[jax.ShapeDtypeStruct((rows, total), arrays[0].dtype)] * cuts,
        grid_spec=pltpu.PrefetchScalarGridSpec(
            num_scalar_prefetch=1,
            grid=(1,),
            in_specs=[spec(c) for c in range(cuts) for _ in range(count)]
            + [pl.BlockSpec(memory_space=pl.ANY)] * len(after),
            out_specs=[pl.BlockSpec((rows, total), lambda i, columns: (0, 0))] * cuts,
        ),
        compiler_params=pltpu.CompilerParams(vmem_limit_bytes=VMEM),
        cost_estimate=pl.CostEstimate(
            flops=0, bytes_accessed=4 * rows * total * cuts, transcendentals=0
        ),
        name="cut",
    )(columns, *(list(arrays) * cuts), *after)


def join(first, second, after=()):
    rows, width = first.shape

    def kernel(first_ref, second_ref, *refs):
        refs[-1][:rows] = first_ref[...]
        refs[-1][rows:] = second_ref[...]

    return pl.pallas_call(
        kernel,
        out_shape=jax.ShapeDtypeStruct((2 * rows, width), first.dtype),
        in_specs=[pl.BlockSpec(memory_space=pltpu.VMEM)] * 2
        + [pl.BlockSpec(memory_space=pl.ANY)] * len(after),
        out_specs=pl.BlockSpec(memory_space=pltpu.VMEM),
        compiler_params=pltpu.CompilerParams(vmem_limit_bytes=VMEM),
        cost_estimate=pl.CostEstimate(
            flops=0, bytes_accessed=8 * rows * width, transcendentals=0
        ),
        name="join",
    )(first, second, *after)


def project(weight, order, tokens, hidden, gate):
    parts, channels, depth = weight.shape
    rows = hidden.shape[0]
    block, each = 512, len(tokens) // parts

    def kernel(order_ref, *refs):
        weight_refs, token_refs = refs[:parts], refs[parts : parts + len(tokens)]
        hidden_ref, gate_ref, out_ref = refs[parts + len(tokens) :]
        total = None
        for part in range(parts):
            mine = [ref[...] for ref in token_refs[part * each : (part + 1) * each]]
            term = lax.dot_general(
                mine[0] if each == 1 else jnp.concatenate(mine, axis=1),
                weight_refs[part][...],
                (((1,), (1,)), ((), ())),
                preferred_element_type=jnp.float32,
            )
            total = term if total is None else total + term
        out_ref[...] = (hidden_ref[...].astype(jnp.float32) + gate_ref[...] * total).astype(
            jnp.bfloat16
        )

    def weight_spec(part):
        return pl.BlockSpec((None, block, depth), lambda j, order: (order[part], j, 0))

    return pl.pallas_call(
        kernel,
        out_shape=jax.ShapeDtypeStruct((rows, channels), jnp.bfloat16),
        grid_spec=pltpu.PrefetchScalarGridSpec(
            num_scalar_prefetch=1,
            grid=(channels // block,),
            in_specs=[weight_spec(part) for part in range(parts)]
            + [pl.BlockSpec(t.shape, lambda j, order: (0, 0)) for t in tokens]
            + [
                pl.BlockSpec((rows, block), lambda j, order: (0, j)),
                pl.BlockSpec((1, block), lambda j, order: (0, j)),
            ],
            out_specs=pl.BlockSpec((rows, block), lambda j, order: (0, j)),
        ),
        compiler_params=pltpu.CompilerParams(vmem_limit_bytes=VMEM),
        cost_estimate=pl.CostEstimate(
            flops=2 * rows * channels * parts * depth,
            bytes_accessed=2 * (channels * parts * depth + 3 * rows * channels),
            transcendentals=0,
        ),
        name="project",
    )(order, *([weight] * parts), *tokens, hidden, gate)


def neighbours(block):
    count = lax.axis_size("fsdp")
    forward = [(i, i + 1) for i in range(count - 1)]
    backward = [(target, source) for source, target in forward]
    return lax.ppermute(block, "fsdp", forward), lax.ppermute(block, "fsdp", backward)


def gathered_weight(out_weight):
    parts = lax.axis_size("seq")
    gathered = lax.all_gather(out_weight.T, ("seq", "fsdp"), axis=0, tiled=True)
    return gathered.reshape(parts, -1, gathered.shape[1])


def pair_block(query, keys, values, picks, live_slots, weight, hidden, gate):
    seat = lax.axis_index("seq").astype(jnp.int32)
    half = query.shape[1] // 2
    width = half // GROUPS
    swap = [(0, 1), (1, 0)]
    order = jnp.stack([seat, 1 - seat])

    place = (picks // 2) * 2 + (picks % 2 != seat).astype(jnp.int32)
    place = jnp.where(seat == 0, place[::-1], place)
    counts = jnp.where(seat == 0, live_slots[::-1], live_slots)
    arrived, theirs, mine, back = [], [], [], []
    zero = jnp.zeros((1,), jnp.int32)
    for group in range(GROUPS):
        last = group == GROUPS - 1
        columns = order * GROUPS + group
        after = (arrived[group - 2],) if group >= 2 else ()
        kv_mine, kv_send = cut([keys, values], columns, width, after)
        kv_other = lax.ppermute(kv_send, "seq", swap)
        arrived.append(kv_other)
        if group < SPLIT:
            before_mine, after_mine = neighbours(kv_mine)
            before_other, after_other = neighbours(kv_other)
            pieces = [before_mine, before_other, kv_mine, kv_other, after_mine, after_other]
        else:
            kv_span = join(kv_mine, kv_other, ((mine if last else theirs)[group - 2],) if group >= 2 else ())
            span_before, span_after = neighbours(kv_span)
            pieces = [span_before, kv_span, span_after]

        (q_send,) = cut([query], columns[1:], width, (theirs[-1] if last else kv_other,))
        q_other = lax.ppermute(q_send, "seq", swap)
        after = tuple(mine[-1:]) + tuple(back[group - 2 : group - 1] if group >= 2 else ())
        (out_other,) = attend([q_other], zero, pieces, place[:1], counts[:1], after)
        back.append(lax.ppermute(out_other, "seq", swap))
        theirs.append(out_other)
        (out_mine,) = attend(
            [query], columns[:1], pieces, place[1:], counts[1:], (out_other,)
        )
        mine.append(out_mine)
    return project(weight, order, mine + back, hidden, gate)


def group_block(query, keys, values, picks, live_slots, weight, hidden, gate):
    parts = lax.axis_size("seq")

    def to_heads(array):
        return lax.all_to_all(array, "seq", split_axis=1, concat_axis=0, tiled=True)

    q_local = to_heads(query)
    kv = jnp.concatenate([to_heads(keys), to_heads(values)], axis=1)
    before, after = neighbours(kv)
    tiles = q_local.shape[0] // TILE
    pieces = [before, kv, after]
    queries = [lax.slice_in_dim(q_local, t * TILE, (t + 1) * TILE) for t in range(tiles)]
    outs = attend(queries, jnp.zeros((tiles,), jnp.int32), pieces, picks, live_slots)
    tokens = lax.all_to_all(
        jnp.concatenate(outs, axis=0), "seq", split_axis=0, concat_axis=1, tiled=True
    )
    width = tokens.shape[1] // parts
    tokens = [lax.slice_in_dim(tokens, p * width, (p + 1) * width, axis=1) for p in range(parts)]
    return project(weight, jnp.arange(parts, dtype=jnp.int32), tokens, hidden, gate)


def on_device(query, keys, values, hidden_in, gate, out_weight, tile_list, tile_count):
    parts = lax.axis_size("seq")
    tiles = query.shape[1] * parts // TILE
    picks = tile_list[0] - (lax.axis_index("fsdp") - 1) * tiles
    paired = parts == 2 and tiles == 2 and query.shape[2] % (2 * GROUPS * HEAD_DIM) == 0
    weight = gathered_weight(out_weight)
    block = pair_block if paired else group_block
    out = block(
        query[0], keys[0], values[0], picks, tile_count[0], weight, hidden_in[0], gate[None, :]
    )
    return out[None]


def solution(mesh):
    return jax.shard_map(
        on_device,
        mesh=mesh,
        in_specs=(
            P("fsdp", "seq", None),
            P("fsdp", "seq", None),
            P("fsdp", "seq", None),
            P("fsdp", "seq", None),
            P(),
            P("seq", "fsdp"),
            P("fsdp", None, None),
            P("fsdp", None),
        ),
        out_specs=P("fsdp", "seq", None),
        check_vma=False,
    )
```

```python
import functools

import jax
import jax.numpy as jnp
from jax import lax
from jax.experimental import pallas as pl
from jax.experimental.pallas import tpu as pltpu
from jax.sharding import PartitionSpec as P

HEAD_DIM = 128
TILE = 512
KMAX = 4
GROUPS = 4
SPLIT = 2
ROWS = 256
VMEM = 60 * 1024 * 1024


def attend_kernel(tiles, heads, pieces, sources, waits, picks_ref, count_ref, column_ref, *refs):
    q_refs, kv_refs = refs[:tiles], refs[tiles : tiles + pieces]
    out_refs, (kv_sel, sems) = refs[tiles + pieces + waits : -2], refs[-2:]
    width = heads * HEAD_DIM
    scale = HEAD_DIM**-0.5 * 1.4426950408889634


    def slot_copy(tile, slot, piece):
        array, row = sources[piece]
        return pltpu.make_async_copy(
            kv_refs[array].at[pl.ds(row, TILE)],
            kv_sel.at[tile, pl.ds(slot * TILE, TILE)],
            sems.at[tile, slot],
        )

    for tile in range(tiles):
        for slot in range(KMAX):
            for piece in range(len(sources)):

                @pl.when((picks_ref[tile, slot] == piece) & (slot < count_ref[tile]))
                def _():
                    slot_copy(tile, slot, piece).start()

    for tile in range(tiles):
        for slot in range(KMAX):

            @pl.when(slot < count_ref[tile])
            def _():
                slot_copy(tile, slot, 0).wait()

        for live in range(2, KMAX + 1):

            @pl.when(count_ref[tile] == live)
            def _():
                for head in range(heads):
                    cols = slice(head * HEAD_DIM, (head + 1) * HEAD_DIM)
                    v_cols = slice(width + head * HEAD_DIM, width + (head + 1) * HEAD_DIM)
                    ones = jnp.ones((live * TILE, HEAD_DIM), jnp.bfloat16)
                    with_ones = jnp.concatenate([kv_sel[tile, : live * TILE, v_cols], ones], axis=1)
                    for block in range(TILE // ROWS):
                        rows = slice(block * ROWS, (block + 1) * ROWS)
                        scores = lax.dot_general(
                            q_refs[tile][rows, cols],
                            kv_sel[tile, : live * TILE, cols],
                            (((1,), (1,)), ((), ())),
                            preferred_element_type=jnp.float32,
                        )
                        row_max = jnp.max(scores, axis=1, keepdims=True)
                        weights = jnp.exp2((scores - row_max) * scale)
                        blended = jnp.dot(
                            weights.astype(jnp.bfloat16),
                            with_ones,
                            preferred_element_type=jnp.float32,
                        )
                        out_refs[tile][rows, cols] = (
                            blended[:, :HEAD_DIM] / blended[:, HEAD_DIM:]
                        ).astype(jnp.bfloat16)


def attend(queries, columns, kv_pieces, picks, counts, after=()):
    tiles, pieces = len(queries), len(kv_pieces)
    sources = [
        (n, row) for n, piece in enumerate(kv_pieces) for row in range(0, piece.shape[0], TILE)
    ]
    width = kv_pieces[0].shape[1] // 2
    heads = width // HEAD_DIM

    def q_spec(tile):
        return pl.BlockSpec((TILE, width), lambda i, picks, count, column: (0, column[tile]))

    whole = pl.BlockSpec((TILE, width), lambda i, picks, count, column: (0, 0))
    return pl.pallas_call(
        functools.partial(attend_kernel, tiles, heads, pieces, sources, len(after)),
        out_shape=[jax.ShapeDtypeStruct((TILE, width), jnp.bfloat16)] * tiles,
        grid_spec=pltpu.PrefetchScalarGridSpec(
            num_scalar_prefetch=3,
            grid=(1,),
            in_specs=[q_spec(tile) for tile in range(tiles)]
            + [pl.BlockSpec(memory_space=pl.ANY)] * (pieces + len(after)),
            out_specs=[whole] * tiles,
            scratch_shapes=[
                pltpu.VMEM((tiles, KMAX * TILE, 2 * width), jnp.bfloat16),
                pltpu.SemaphoreType.DMA((tiles, KMAX)),
            ],
        ),
        compiler_params=pltpu.CompilerParams(vmem_limit_bytes=VMEM),
        cost_estimate=pl.CostEstimate(
            flops=4 * tiles * TILE * KMAX * TILE * width,
            bytes_accessed=2 * TILE * width * tiles * (2 * KMAX + 2),
            transcendentals=tiles * TILE * KMAX * TILE * heads,
        ),
        name="attend",
    )(picks, counts, columns, *queries, *kv_pieces, *after)


def cut(arrays, columns, width, after=()):
    count, cuts, rows = len(arrays), columns.shape[0], arrays[0].shape[0]

    def kernel(columns_ref, *refs):
        outs = refs[cuts * count + len(after) :]
        for c in range(cuts):
            for n in range(count):
                outs[c][:, n * width : (n + 1) * width] = refs[c * count + n][...]

    def spec(c):
        return pl.BlockSpec((rows, width), lambda i, columns: (0, columns[c]))

    total = width * count
    return pl.pallas_call(
        kernel,
        out_shape=[jax.ShapeDtypeStruct((rows, total), arrays[0].dtype)] * cuts,
        grid_spec=pltpu.PrefetchScalarGridSpec(
            num_scalar_prefetch=1,
            grid=(1,),
            in_specs=[spec(c) for c in range(cuts) for _ in range(count)]
            + [pl.BlockSpec(memory_space=pl.ANY)] * len(after),
            out_specs=[pl.BlockSpec((rows, total), lambda i, columns: (0, 0))] * cuts,
        ),
        compiler_params=pltpu.CompilerParams(vmem_limit_bytes=VMEM),
        cost_estimate=pl.CostEstimate(
            flops=0, bytes_accessed=4 * rows * total * cuts, transcendentals=0
        ),
        name="cut",
    )(columns, *(list(arrays) * cuts), *after)


def join(first, second, after=()):
    rows, width = first.shape

    def kernel(first_ref, second_ref, *refs):
        refs[-1][:rows] = first_ref[...]
        refs[-1][rows:] = second_ref[...]

    return pl.pallas_call(
        kernel,
        out_shape=jax.ShapeDtypeStruct((2 * rows, width), first.dtype),
        in_specs=[pl.BlockSpec(memory_space=pltpu.VMEM)] * 2
        + [pl.BlockSpec(memory_space=pl.ANY)] * len(after),
        out_specs=pl.BlockSpec(memory_space=pltpu.VMEM),
        compiler_params=pltpu.CompilerParams(vmem_limit_bytes=VMEM),
        cost_estimate=pl.CostEstimate(
            flops=0, bytes_accessed=8 * rows * width, transcendentals=0
        ),
        name="join",
    )(first, second, *after)


def project(weight, order, tokens, hidden, gate):
    parts, channels, depth = weight.shape
    rows = hidden.shape[0]
    block, each = 512, len(tokens) // parts

    def kernel(order_ref, *refs):
        weight_refs, token_refs = refs[:parts], refs[parts : parts + len(tokens)]
        hidden_ref, gate_ref, out_ref = refs[parts + len(tokens) :]
        total = None
        for part in range(parts):
            mine = [ref[...] for ref in token_refs[part * each : (part + 1) * each]]
            term = lax.dot_general(
                mine[0] if each == 1 else jnp.concatenate(mine, axis=1),
                weight_refs[part][...],
                (((1,), (1,)), ((), ())),
                preferred_element_type=jnp.float32,
            )
            total = term if total is None else total + term
        out_ref[...] = (hidden_ref[...].astype(jnp.float32) + gate_ref[...] * total).astype(
            jnp.bfloat16
        )

    def weight_spec(part):
        return pl.BlockSpec((None, block, depth), lambda j, order: (order[part], j, 0))

    return pl.pallas_call(
        kernel,
        out_shape=jax.ShapeDtypeStruct((rows, channels), jnp.bfloat16),
        grid_spec=pltpu.PrefetchScalarGridSpec(
            num_scalar_prefetch=1,
            grid=(channels // block,),
            in_specs=[weight_spec(part) for part in range(parts)]
            + [pl.BlockSpec(t.shape, lambda j, order: (0, 0)) for t in tokens]
            + [
                pl.BlockSpec((rows, block), lambda j, order: (0, j)),
                pl.BlockSpec((1, block), lambda j, order: (0, j)),
            ],
            out_specs=pl.BlockSpec((rows, block), lambda j, order: (0, j)),
        ),
        compiler_params=pltpu.CompilerParams(vmem_limit_bytes=VMEM),
        cost_estimate=pl.CostEstimate(
            flops=2 * rows * channels * parts * depth,
            bytes_accessed=2 * (channels * parts * depth + 3 * rows * channels),
            transcendentals=0,
        ),
        name="project",
    )(order, *([weight] * parts), *tokens, hidden, gate)


def neighbours(block):
    count = lax.axis_size("fsdp")
    forward = [(i, i + 1) for i in range(count - 1)]
    backward = [(target, source) for source, target in forward]
    return lax.ppermute(block, "fsdp", forward), lax.ppermute(block, "fsdp", backward)


def gathered_weight(out_weight):
    parts = lax.axis_size("seq")
    gathered = lax.all_gather(out_weight.T, ("seq", "fsdp"), axis=0, tiled=True)
    return gathered.reshape(parts, -1, gathered.shape[1])


def pair_block(query, keys, values, picks, live_slots, weight, hidden, gate):
    seat = lax.axis_index("seq").astype(jnp.int32)
    half = query.shape[1] // 2
    width = half // GROUPS
    swap = [(0, 1), (1, 0)]
    order = jnp.stack([seat, 1 - seat])

    place = (picks // 2) * 2 + (picks % 2 != seat).astype(jnp.int32)
    place = jnp.where(seat == 0, place[::-1], place)
    counts = jnp.where(seat == 0, live_slots[::-1], live_slots)
    arrived, theirs, mine, back = [], [], [], []
    zero = jnp.zeros((1,), jnp.int32)
    for group in range(GROUPS):
        last = group == GROUPS - 1
        columns = order * GROUPS + group
        after = (arrived[group - 2],) if group >= 2 else ()
        kv_mine, kv_send = cut([keys, values], columns, width, after)
        kv_other = lax.ppermute(kv_send, "seq", swap)
        arrived.append(kv_other)
        if group < SPLIT:
            before_mine, after_mine = neighbours(kv_mine)
            before_other, after_other = neighbours(kv_other)
            pieces = [before_mine, before_other, kv_mine, kv_other, after_mine, after_other]
        else:
            kv_span = join(kv_mine, kv_other, ((mine if last else theirs)[group - 2],) if group >= 2 else ())
            span_before, span_after = neighbours(kv_span)
            pieces = [span_before, kv_span, span_after]

        (q_send,) = cut([query], columns[1:], width, (theirs[-1] if last else kv_other,))
        q_other = lax.ppermute(q_send, "seq", swap)
        after = tuple(mine[-1:]) + tuple(back[group - 2 : group - 1] if group >= 2 else ())
        (out_other,) = attend([q_other], zero, pieces, place[:1], counts[:1], after)
        back.append(lax.ppermute(out_other, "seq", swap))
        theirs.append(out_other)
        (out_mine,) = attend(
            [query], columns[:1], pieces, place[1:], counts[1:], (out_other,)
        )
        mine.append(out_mine)
    return project(weight, order, mine + back, hidden, gate)


def group_block(query, keys, values, picks, live_slots, weight, hidden, gate):
    parts = lax.axis_size("seq")

    def to_heads(array):
        return lax.all_to_all(array, "seq", split_axis=1, concat_axis=0, tiled=True)

    q_local = to_heads(query)
    kv = jnp.concatenate([to_heads(keys), to_heads(values)], axis=1)
    before, after = neighbours(kv)
    tiles = q_local.shape[0] // TILE
    pieces = [before, kv, after]
    queries = [lax.slice_in_dim(q_local, t * TILE, (t + 1) * TILE) for t in range(tiles)]
    outs = attend(queries, jnp.zeros((tiles,), jnp.int32), pieces, picks, live_slots)
    tokens = lax.all_to_all(
        jnp.concatenate(outs, axis=0), "seq", split_axis=0, concat_axis=1, tiled=True
    )
    width = tokens.shape[1] // parts
    tokens = [lax.slice_in_dim(tokens, p * width, (p + 1) * width, axis=1) for p in range(parts)]
    return project(weight, jnp.arange(parts, dtype=jnp.int32), tokens, hidden, gate)


def on_device(query, keys, values, hidden_in, gate, out_weight, tile_list, tile_count):
    parts = lax.axis_size("seq")
    tiles = query.shape[1] * parts // TILE
    picks = tile_list[0] - (lax.axis_index("fsdp") - 1) * tiles
    paired = parts == 2 and tiles == 2 and query.shape[2] % (2 * GROUPS * HEAD_DIM) == 0
    weight = gathered_weight(out_weight)
    block = pair_block if paired else group_block
    out = block(
        query[0], keys[0], values[0], picks, tile_count[0], weight, hidden_in[0], gate[None, :]
    )
    return out[None]


def solution(mesh):
    return jax.shard_map(
        on_device,
        mesh=mesh,
        in_specs=(
            P("fsdp", "seq", None),
            P("fsdp", "seq", None),
            P("fsdp", "seq", None),
            P("fsdp", "seq", None),
            P(),
            P("seq", "fsdp"),
            P("fsdp", None, None),
            P("fsdp", None),
        ),
        out_specs=P("fsdp", "seq", None),
        check_vma=False,
    )
```
